128 devices in a mesh: lb: 8 (over z_lo, x), rb: 16 (over z_hi, y, core).
Axes of the slice: x: 4, y: 4, z: 4 (z_hi: 2, z_lo: 2; z = z_hi * 2 + z_lo), core: 2. Of those that a mesh axis runs over, the one named last changes fastest.
Arguments:
- psi: bfloat16 [16384, 8192], P('lb', 'rb'), may hold values from -6 to 6
- left_env: bfloat16 [28, 16384, 128], P(None, 'lb'), may hold values from -0.5 to 0.5
- right_env: bfloat16 [28, 8192, 128], P(None, 'rb'), may hold values from -0.09375 to 0.09375
- left_src: int32 [28, 128], replicated, may hold values from 0 to 127, as said below
- right_dst: int32 [28, 64], replicated, may hold values from 0 to 63, as said below
Outputs:
- h_psi: bfloat16 [16384, 8192], P('lb', 'rb')
The draws below stay inside these ranges and needn't reach their ends.
Inputs may be any that keep to these rules, and one draw needn't show every extreme that they name: `left_src`: each entry differs from its block index i by at most 2, and that distance is reached. `right_dst`: each entry differs from its block index j by at most 2, and that distance is reached.
All inputs are finite; a program needn't handle non-finite values.
Results may differ from the reference program's by a relative error of at most 0.0049.
Values may be sent and summed in bfloat16 or wider, within the bound.
A program may use at most 128 MiB of HBM per device.

```python
import jax
import jax.numpy as jnp
from jax import lax

BLOCK = 128
NW = 28
SPAN = 2
NBL = 128
NBR = 64
ML = 16384
MR = 8192


def bounded_shift(key, count):
    shifts = jax.random.randint(key, (NW, count), -SPAN, SPAN + 1).astype(jnp.int32)
    places = jnp.arange(count, dtype=jnp.int32)[None, :] + shifts
    places = jnp.clip(places, 0, count - 1)
    middle = count // 2
    return places.at[0, middle].set(middle + SPAN).astype(jnp.int32)


def draw_left_src(key, part):
    key = jax.random.fold_in(key, 11)
    return bounded_shift(key, NBL)


def draw_right_dst(key, part):
    key = jax.random.fold_in(key, 23)
    return bounded_shift(key, NBR)


def level_of(key, shape, cuts, low, largest):
    def one(position, parts):
        steps = jax.random.uniform(jax.random.fold_in(jax.random.fold_in(key, 6), position), (parts,), jnp.float32, low / len(cuts), largest / len(cuts))
        return jnp.repeat(jnp.exp(steps), shape[position] // parts).reshape((-1,) + (1,) * (len(shape) - position - 1))

    factor_of = one(*cuts[0])
    for cut in cuts[1:]:
        factor_of = factor_of * one(*cut)
    return factor_of


def centred(stream_key, dims, scale, most, cuts=(), held_as=jnp.bfloat16):
    drawn = jax.random.normal(stream_key, dims, jnp.float32) * scale
    if len(cuts) > 0:
        drawn = level_of(stream_key, dims, cuts, -0.22, 0.18) * drawn
    return jnp.clip(drawn, min=-most, max=most).astype(held_as)


def setup_inputs(seed: int = 0) -> dict:
    key_list = jax.random.split(jax.random.key(seed), 6)
    psi = centred(key_list[0], (ML, MR), 1.0, 6.0, ((0, 8), (1, 16)))
    left_env = centred(key_list[1], (NW, ML, BLOCK), BLOCK ** -0.5, 0.5, ((1, 8),))
    right_env = centred(key_list[2], (NW, MR, BLOCK), (NW * BLOCK) ** -0.5, 0.09375, ((1, 16),))
    left_src = draw_left_src(jax.random.fold_in(key_list[5], 71), 0)
    right_dst = draw_right_dst(jax.random.fold_in(key_list[5], 71), 0)
    return dict(psi=psi, left_env=left_env, right_env=right_env, left_src=left_src, right_dst=right_dst)


def reference(psi, left_env, right_env, left_src, right_dst):
    row_blocks = psi.astype(jnp.float32).reshape(NBL, BLOCK, MR)
    left_blocks = left_env.astype(jnp.float32).reshape(NW, NBL, BLOCK, BLOCK)
    right_blocks = right_env.astype(jnp.float32).reshape(NW, NBR, BLOCK, BLOCK)

    def apply_term(term_index, totals):
        picked = jnp.take(row_blocks, left_src[term_index], axis=0)
        inner = jnp.einsum('irc,icm->irm', left_blocks[term_index], picked)
        inner = lax.optimization_barrier(inner.astype(jnp.bfloat16)).astype(jnp.float32)
        inner = inner.reshape(ML, NBR, BLOCK)
        contrib = jnp.einsum('mjc,jce->mje', inner, right_blocks[term_index])
        return totals.at[:, right_dst[term_index]].add(contrib)

    totals = lax.fori_loop(0, NW, apply_term, jnp.zeros((ML, NBR, BLOCK), jnp.float32))
    return totals.reshape(ML, MR).astype(jnp.bfloat16)
```

```python
import functools

import jax
import jax.numpy as jnp
from jax import lax
from jax.experimental import pallas as pl
from jax.experimental.pallas import tpu as pltpu
from jax.sharding import PartitionSpec as P

SPAN = 2
B = 128
GROUP = 4
CHUNK = 4
MESH = pl.DeviceIdType.MESH
BF = jnp.bfloat16
F32 = jnp.float32


def max_groups(entries, targets):
    return (entries + (GROUP - 1) * targets) // GROUP


def plan_kernel(terms, right_count, dst_ref, entry_ref, factor_ref, joined_ref, last_ref, count, bucket):
    start = lax.axis_index("rb") * right_count
    targets = right_count + 2 * SPAN
    entries = terms * right_count
    groups = max_groups(entries, targets)
    for d in range(targets):
        count[d] = 0

    def place(w, carry):
        for j in range(right_count):
            d = dst_ref[w, start + j] - start + SPAN
            n = count[d]
            bucket[d * entries + n] = w * right_count + j
            count[d] = n + 1
        return carry

    lax.fori_loop(0, terms, place, 0)

    def blank(g, carry):
        for q in range(GROUP):
            entry_ref[GROUP * g + q] = 0
            factor_ref[GROUP * g + q] = entries
        joined_ref[g] = 0
        return carry

    used = jnp.int32(0)
    for d in range(targets):
        n = count[d]
        parts = (n + GROUP - 1) // GROUP

        def emit(k, g):
            for q in range(GROUP):
                at = GROUP * k + q
                here = at < n
                e = bucket[d * entries + jnp.minimum(at, entries - 1)]
                entry_ref[GROUP * g + q] = jnp.where(here, e, 0)
                factor_ref[GROUP * g + q] = jnp.where(here, e, entries)
            joined_ref[g] = (k > 0).astype(jnp.int32)
            return g + 1

        used = lax.fori_loop(0, parts, emit, used)
        last_ref[d] = jnp.where(n > 0, used - 1, groups)
    lax.fori_loop(used, groups, blank, 0)


def main_kernel(
    sizes, src_ref, entry_ref, factor_ref, joined_ref, last_ref, psi, left, right, out,
    psi_v, low_v, high_v, psi_t, right_v, right_t, left_v, inner, slots,
    send_down, send_up, from_below, from_above, out_v,
    psi_sem, right_sem, left_sem, out_sem, halo_send, halo_recv, edge_send, edge_recv,
):
    lb_size, rb_size, terms, left_count, right_count = sizes
    targets = right_count + 2 * SPAN
    entries = terms * right_count
    groups = max_groups(entries, targets)
    rows, cols = left_count * B, right_count * B
    width = CHUNK * B
    chunks = left_count // CHUNK
    halo = SPAN * B
    a, b = lax.axis_index("lb"), lax.axis_index("rb")
    neighbours = (
        (a > 0, {"lb": a - 1}), (a < lb_size - 1, {"lb": a + 1}),
        (b > 0, {"rb": b - 1}), (b < rb_size - 1, {"rb": b + 1}),
    )

    psi_copy = pltpu.make_async_copy(psi, psi_v, psi_sem)
    right_copy = pltpu.make_async_copy(right, right_v, right_sem)

    def rows_of(c, p):
        return pl.multiple_of(lax.rem(halo + c * width + p * 2 * B, rows), 2 * B)

    def left_copy(c, p):
        return pltpu.make_async_copy(
            left.at[:, pl.ds(rows_of(c, p), 2 * B)],
            left_v.at[lax.rem(c, 2), :, pl.ds(p * 2 * B, 2 * B)],
            left_sem.at[lax.rem(c, 2), p],
        )

    def out_copy(c, p):
        at = pl.ds(rows_of(c, p), 2 * B)
        return pltpu.make_async_copy(out_v.at[at], out.at[at], out_sem.at[c, p])

    def halo_copy(side):
        if side == 0:
            return pltpu.make_async_remote_copy(
                src_ref=psi.at[pl.ds(0, halo)], dst_ref=high_v, send_sem=halo_send.at[0],
                recv_sem=halo_recv.at[0], device_id={"lb": a - 1}, device_id_type=MESH)
        return pltpu.make_async_remote_copy(
            src_ref=psi.at[pl.ds(rows - halo, halo)], dst_ref=low_v, send_sem=halo_send.at[1],
            recv_sem=halo_recv.at[1], device_id={"lb": a + 1}, device_id_type=MESH)

    def edge_copy(c, side):
        if side == 0:
            return pltpu.make_async_remote_copy(
                src_ref=send_down.at[c], dst_ref=from_above.at[c], send_sem=edge_send.at[0, c],
                recv_sem=edge_recv.at[0, c], device_id={"rb": b - 1}, device_id_type=MESH)
        return pltpu.make_async_remote_copy(
            src_ref=send_up.at[c], dst_ref=from_below.at[c], send_sem=edge_send.at[1, c],
            recv_sem=edge_recv.at[1, c], device_id={"rb": b + 1}, device_id_type=MESH)

    psi_copy.start()
    right_copy.start()
    for p in range(2):
        left_copy(0, p).start()

    barrier = pltpu.get_barrier_semaphore()
    for there, device in neighbours:
        @pl.when(there)
        def _():
            pl.semaphore_signal(barrier, inc=1, device_id=device, device_id_type=MESH)
    pl.semaphore_wait(barrier, sum(there.astype(jnp.int32) for there, _ in neighbours))

    @pl.when(a > 0)
    def _():
        halo_copy(0).start()

    @pl.when(a < lb_size - 1)
    def _():
        halo_copy(1).start()

    @pl.when(b == 0)
    def _():
        from_below[...] = jnp.zeros_like(from_below)

    @pl.when(b == rb_size - 1)
    def _():
        from_above[...] = jnp.zeros_like(from_above)

    right_t[entries] = jnp.zeros((B, B), BF)
    slots[groups] = jnp.zeros((B, width), F32)

    psi_copy.wait()

    def turn_psi(s, carry):
        for u in range(4):
            at = pl.multiple_of((4 * s + u) * B, B)
            psi_t[4 * s + u + SPAN] = psi_v[pl.ds(at, B), :].T
        return carry

    lax.fori_loop(0, left_count // 4, turn_psi, 0)
    right_copy.wait()

    def turn_right(w, carry):
        for u in range(4):
            for j in range(right_count):
                right_t[(4 * w + u) * right_count + j] = right_v[4 * w + u, pl.ds(j * B, B), :].T
        return carry

    lax.fori_loop(0, terms // 4, turn_right, 0)

    zero = jnp.zeros((B, B), BF)

    def finish(c):
        @pl.when(b > 0)
        def _():
            edge_copy(c, 1).wait_recv()

        @pl.when(b < rb_size - 1)
        def _():
            edge_copy(c, 0).wait_recv()

        for j in range(right_count):
            mine = slots[last_ref[SPAN + j]]
            if j < SPAN:
                mine = mine + from_below[c, pl.ds(j * B, B), :].astype(F32)
            if j >= right_count - SPAN:
                mine = mine + from_above[c, pl.ds((j - right_count + SPAN) * B, B), :].astype(F32)
            turned = mine.astype(BF).T
            for p in range(2):
                out_v[pl.ds(rows_of(c, p), 2 * B), pl.ds(j * B, B)] = turned[p * 2 * B : (p + 1) * 2 * B]
        for p in range(2):
            out_copy(c, p).start()

    def step(c, carry):
        for p in range(2):
            left_copy(c, p).wait()

        @pl.when(c < chunks - 1)
        def _():
            for p in range(2):
                left_copy(c + 1, p).start()

        @pl.when(c == chunks - 1)
        def _():
            @pl.when(a > 0)
            def _():
                halo_copy(1).wait_recv()
                for k in range(SPAN):
                    psi_t[k] = low_v[pl.ds(k * B, B), :].T

            @pl.when(a < lb_size - 1)
            def _():
                halo_copy(0).wait_recv()
                for k in range(SPAN):
                    psi_t[SPAN + left_count + k] = high_v[pl.ds(k * B, B), :].T

        first = a * left_count
        slot = lax.rem(c, 2)
        for w in range(terms):
            for p in range(2):
                i = first + lax.rem(SPAN + c * CHUNK + 2 * p, left_count)
                shift = SPAN - first
                x = jnp.concatenate(
                    [psi_t[jnp.clip(src_ref[w, i + k] + shift, 0, left_count + 2 * SPAN - 1)] for k in range(2)],
                    axis=1)
                upper = left_v[slot, w, pl.ds(p * 2 * B, B), :].T
                lower = left_v[slot, w, pl.ds(p * 2 * B + B, B), :].T
                both = jnp.concatenate(
                    [jnp.concatenate([upper, zero], axis=1), jnp.concatenate([zero, lower], axis=1)], axis=0)
                y = jnp.dot(x, both, preferred_element_type=F32).astype(BF)
                for j in range(right_count):
                    inner[w * right_count + j, :, pl.ds(p * 2 * B, 2 * B)] = y[j * B : (j + 1) * B]

        @pl.when(c > 0)
        def _():
            finish(c - 1)

        for g in range(groups):
            k = jnp.concatenate([inner[entry_ref[GROUP * g + q]] for q in range(GROUP)], axis=0)
            r = jnp.concatenate([right_t[factor_ref[GROUP * g + q]] for q in range(GROUP)], axis=1)
            y = jnp.dot(r, k, preferred_element_type=F32)
            if g > 0:
                y = y + jnp.where(joined_ref[g] == 1, slots[g - 1], 0.0)
            slots[g] = y
        for k in range(SPAN):
            send_down[c, pl.ds(k * B, B), :] = slots[last_ref[k]].astype(BF)
            send_up[c, pl.ds(k * B, B), :] = slots[last_ref[SPAN + right_count + k]].astype(BF)

        @pl.when(b > 0)
        def _():
            edge_copy(c, 0).start()

        @pl.when(b < rb_size - 1)
        def _():
            edge_copy(c, 1).start()
        return carry

    lax.fori_loop(0, chunks, step, 0)
    finish(chunks - 1)

    def drain(c, carry):
        for p in range(2):
            out_copy(c, p).wait()

        @pl.when(b > 0)
        def _():
            edge_copy(c, 0).wait_send()

        @pl.when(b < rb_size - 1)
        def _():
            edge_copy(c, 1).wait_send()
        return carry

    lax.fori_loop(0, chunks, drain, 0)

    @pl.when(a > 0)
    def _():
        halo_copy(0).wait_send()

    @pl.when(a < lb_size - 1)
    def _():
        halo_copy(1).wait_send()


def on_device(lb_size, rb_size, psi, left_env, right_env, left_src, right_dst):
    rows, cols = psi.shape
    terms = left_env.shape[0]
    left_count, right_count = rows // B, cols // B
    entries, targets = terms * right_count, right_count + 2 * SPAN
    groups = max_groups(entries, targets)
    chunks, width, halo = left_count // CHUNK, CHUNK * B, SPAN * B
    smem = pl.BlockSpec(memory_space=pltpu.SMEM)
    hbm = pl.BlockSpec(memory_space=pl.ANY)
    ints = lambda n: jax.ShapeDtypeStruct((n,), jnp.int32)
    plan = pl.pallas_call(
        functools.partial(plan_kernel, terms, right_count),
        out_shape=(ints(GROUP * groups), ints(GROUP * groups), ints(groups), ints(targets)),
        in_specs=[smem],
        out_specs=(smem,) * 4,
        scratch_shapes=[pltpu.SMEM((targets,), jnp.int32), pltpu.SMEM((targets * entries,), jnp.int32)],
        name="plan",
    )(right_dst)
    dma = pltpu.SemaphoreType.DMA
    return pl.pallas_call(
        functools.partial(main_kernel, (lb_size, rb_size, terms, left_count, right_count)),
        out_shape=jax.ShapeDtypeStruct((rows, cols), BF),
        in_specs=[smem] * 5 + [hbm] * 3,
        out_specs=hbm,
        scratch_shapes=[
            pltpu.VMEM((rows, cols), BF),
            pltpu.VMEM((halo, cols), BF),
            pltpu.VMEM((halo, cols), BF),
            pltpu.VMEM((left_count + 2 * SPAN, cols, B), BF),
            pltpu.VMEM((terms, cols, B), BF),
            pltpu.VMEM((entries + 1, B, B), BF),
            pltpu.VMEM((2, terms, width, B), BF),
            pltpu.VMEM((entries, B, width), BF),
            pltpu.VMEM((groups + 1, B, width), F32),
            pltpu.VMEM((chunks, halo, width), BF),
            pltpu.VMEM((chunks, halo, width), BF),
            pltpu.VMEM((chunks, halo, width), BF),
            pltpu.VMEM((chunks, halo, width), BF),
            pltpu.VMEM((rows, cols), BF),
            dma(()), dma(()), dma((2, 2)), dma((chunks, 2)), dma((2,)), dma((2,)), dma((2, chunks)), dma((2, chunks)),
        ],
        compiler_params=pltpu.CompilerParams(
            collective_id=0, has_side_effects=True, vmem_limit_bytes=60 * 2**20),
        name="apply",
    )(left_src, *plan, psi, left_env, right_env)


def solution(mesh):
    return jax.shard_map(
        functools.partial(on_device, mesh.shape["lb"], mesh.shape["rb"]),
        mesh=mesh,
        in_specs=(P("lb", "rb"), P(None, "lb", None), P(None, "rb", None), P(), P()),
        out_specs=P("lb", "rb"),
        check_vma=False,
    )
```

```python
import functools

import jax
import jax.numpy as jnp
from jax import lax
from jax.experimental import pallas as pl
from jax.experimental.pallas import tpu as pltpu
from jax.sharding import PartitionSpec as P

SPAN = 2
B = 128
GROUP = 4
CHUNK = 4
LISTED = 256
MESH = pl.DeviceIdType.MESH
BF = jnp.bfloat16
F32 = jnp.float32


def max_groups(entries, targets):
    return (entries + (GROUP - 1) * targets) // GROUP


def plan(terms, right_count, start, dst_ref, list_v, last_ref):
    targets = right_count + 2 * SPAN
    entries = terms * right_count
    groups = max_groups(entries, targets)

    def target(w, j):
        return dst_ref[w, start + j] - start + SPAN

    def tally(w, counts):
        for j in range(right_count):
            d = target(w, j)
            counts = tuple(n + (d == k).astype(jnp.int32) for k, n in enumerate(counts))
        return counts

    zeros = (jnp.int32(0),) * targets
    counts = lax.fori_loop(0, terms, tally, zeros)
    place = lax.broadcasted_iota(jnp.int32, (8, B), 0) * B + lax.broadcasted_iota(jnp.int32, (8, B), 1)
    listed = jnp.where(place < LISTED, entries, 1)
    begin = jnp.int32(0)
    begins = []
    for k, n in enumerate(counts):
        begins.append(begin * GROUP)
        listed = jnp.where(place == LISTED + begin, 0, listed)
        begin = begin + (n + GROUP - 1) // GROUP
        last_ref[k] = jnp.where(n > 0, begin - 1, groups)

    def put(w, carry):
        nexts, listed = carry
        for j in range(right_count):
            d = target(w, j)
            at = sum(jnp.where(d == k, n, 0) for k, n in enumerate(nexts))
            nexts = tuple(n + (d == k).astype(jnp.int32) for k, n in enumerate(nexts))
            listed = jnp.where(place == at, w * right_count + j, listed)
        return nexts, listed

    _, listed = lax.fori_loop(0, terms, put, (tuple(begins), listed))
    list_v[...] = listed


def main_kernel(
    sizes, src_ref, dst_ref, psi, left, right, out,
    list_v, list_s, last_ref, psi_v, low_v, high_v, psi_t, right_v, right_t, left_v, inner, slots, held,
    send_down, send_up, from_below, from_above,
    list_sem, psi_sem, right_sem, left_sem, halo_send, halo_recv, edge_send, edge_recv,
):
    lb_size, rb_size, terms, left_count, right_count = sizes
    targets = right_count + 2 * SPAN
    entries = terms * right_count
    groups = max_groups(entries, targets)
    rows, cols = left_count * B, right_count * B
    width = CHUNK * B
    chunks = left_count // CHUNK
    halo = SPAN * B
    a, b = lax.axis_index("lb"), lax.axis_index("rb")
    neighbours = (
        (a > 0, {"lb": a - 1}), (a < lb_size - 1, {"lb": a + 1}),
        (b > 0, {"rb": b - 1}), (b < rb_size - 1, {"rb": b + 1}),
    )

    psi_copy = pltpu.make_async_copy(psi, psi_v, psi_sem)
    right_copy = pltpu.make_async_copy(right, right_v, right_sem)
    list_copy = pltpu.make_async_copy(list_v, list_s, list_sem)

    def rows_of(c, p):
        return pl.multiple_of(lax.rem(halo + c * width + p * 2 * B, rows), 2 * B)

    def left_copy(c, p):
        return pltpu.make_async_copy(
            left.at[:, pl.ds(rows_of(c, p), 2 * B)],
            left_v.at[lax.rem(c, 2), :, pl.ds(p * 2 * B, 2 * B)],
            left_sem.at[lax.rem(c, 2), p],
        )

    def halo_copy(side):
        if side == 0:
            return pltpu.make_async_remote_copy(
                src_ref=psi.at[pl.ds(0, halo)], dst_ref=high_v, send_sem=halo_send.at[0],
                recv_sem=halo_recv.at[0], device_id={"lb": a - 1}, device_id_type=MESH)
        return pltpu.make_async_remote_copy(
            src_ref=psi.at[pl.ds(rows - halo, halo)], dst_ref=low_v, send_sem=halo_send.at[1],
            recv_sem=halo_recv.at[1], device_id={"lb": a + 1}, device_id_type=MESH)

    def edge_copy(c, p, side):
        if side == 0:
            return pltpu.make_async_remote_copy(
                src_ref=send_down.at[c, p], dst_ref=from_above.at[c, p], send_sem=edge_send.at[0, c, p],
                recv_sem=edge_recv.at[0, c, p], device_id={"rb": b - 1}, device_id_type=MESH)
        return pltpu.make_async_remote_copy(
            src_ref=send_up.at[c, p], dst_ref=from_below.at[c, p], send_sem=edge_send.at[1, c, p],
            recv_sem=edge_recv.at[1, c, p], device_id={"rb": b + 1}, device_id_type=MESH)

    psi_copy.start()
    right_copy.start()
    for p in range(2):
        left_copy(0, p).start()

    barrier = pltpu.get_barrier_semaphore()
    for there, device in neighbours:
        @pl.when(there)
        def _():
            pl.semaphore_signal(barrier, inc=1, device_id=device, device_id_type=MESH)
    plan(terms, right_count, b * right_count, dst_ref, list_v, last_ref)
    list_copy.start()
    pl.semaphore_wait(barrier, sum(there.astype(jnp.int32) for there, _ in neighbours))

    @pl.when(a > 0)
    def _():
        halo_copy(0).start()

    @pl.when(a < lb_size - 1)
    def _():
        halo_copy(1).start()

    @pl.when(b == 0)
    def _():
        from_below[...] = jnp.zeros_like(from_below)

    @pl.when(b == rb_size - 1)
    def _():
        from_above[...] = jnp.zeros_like(from_above)

    right_t[entries] = jnp.zeros((B, B), BF)
    slots[groups] = jnp.zeros((B, 2 * B), F32)

    psi_copy.wait()

    def turn_psi(s, carry):
        for u in range(4):
            at = pl.multiple_of((4 * s + u) * B, B)
            psi_t[4 * s + u + SPAN] = psi_v[pl.ds(at, B), :].T
        return carry

    lax.fori_loop(0, left_count // 4, turn_psi, 0)
    right_copy.wait()

    def turn_right(w, carry):
        for u in range(4):
            for j in range(right_count):
                right_t[(4 * w + u) * right_count + j] = right_v[4 * w + u, pl.ds(j * B, B), :].T
        return carry

    lax.fori_loop(0, terms // 4, turn_right, 0)

    zero = jnp.zeros((B, B), BF)

    def finish(c, p):
        @pl.when(b > 0)
        def _():
            edge_copy(c, p, 1).wait_recv()

        @pl.when(b < rb_size - 1)
        def _():
            edge_copy(c, p, 0).wait_recv()

        for j in range(right_count):
            mine = held[p, lax.rem(c, 2), j]
            if j < SPAN:
                mine = mine + from_below[c, p, pl.ds(j * B, B), :].astype(F32)
            if j >= right_count - SPAN:
                mine = mine + from_above[c, p, pl.ds((j - right_count + SPAN) * B, B), :].astype(F32)
            out[pl.ds(rows_of(c, p), 2 * B), pl.ds(j * B, B)] = mine.astype(BF).T

    def step(c, carry):
        for p in range(2):
            left_copy(c, p).wait()

        @pl.when(c < chunks - 1)
        def _():
            for p in range(2):
                left_copy(c + 1, p).start()

        @pl.when(c == chunks - 1)
        def _():
            @pl.when(a > 0)
            def _():
                halo_copy(1).wait_recv()
                for k in range(SPAN):
                    psi_t[k] = low_v[pl.ds(k * B, B), :].T

            @pl.when(a < lb_size - 1)
            def _():
                halo_copy(0).wait_recv()
                for k in range(SPAN):
                    psi_t[SPAN + left_count + k] = high_v[pl.ds(k * B, B), :].T

        first = a * left_count
        slot = lax.rem(c, 2)
        for w in range(terms):
            for p in range(2):
                i = first + lax.rem(SPAN + c * CHUNK + 2 * p, left_count)
                shift = SPAN - first
                x = jnp.concatenate(
                    [psi_t[jnp.clip(src_ref[w, i + k] + shift, 0, left_count + 2 * SPAN - 1)] for k in range(2)],
                    axis=1)
                upper = left_v[slot, w, pl.ds(p * 2 * B, B), :].T
                lower = left_v[slot, w, pl.ds(p * 2 * B + B, B), :].T
                both = jnp.concatenate(
                    [jnp.concatenate([upper, zero], axis=1), jnp.concatenate([zero, lower], axis=1)], axis=0)
                y = jnp.dot(x, both, preferred_element_type=F32).astype(BF)
                for j in range(right_count):
                    inner[w * right_count + j, :, pl.ds(p * 2 * B, 2 * B)] = y[j * B : (j + 1) * B]

        @pl.when(c == 0)
        def _():
            list_copy.wait()

        def pair(n):
            return list_s[n // B, n % B]

        for p in range(2):
            for g in range(groups):
                at = [pair(GROUP * g + q) for q in range(GROUP)]
                k = jnp.concatenate(
                    [inner[jnp.clip(e, 0, entries - 1), :, pl.ds(p * 2 * B, 2 * B)] for e in at], axis=0)
                r = jnp.concatenate([right_t[e] for e in at], axis=1)
                y = jnp.dot(r, k, preferred_element_type=F32)
                if g > 0:
                    y = y + jnp.where(pair(LISTED + g) == 1, slots[g - 1], 0.0)
                slots[g] = y
            for k in range(SPAN):
                send_down[c, p, pl.ds(k * B, B), :] = slots[last_ref[k]].astype(BF)
                send_up[c, p, pl.ds(k * B, B), :] = slots[last_ref[SPAN + right_count + k]].astype(BF)

            @pl.when(b > 0)
            def _():
                edge_copy(c, p, 0).start()

            @pl.when(b < rb_size - 1)
            def _():
                edge_copy(c, p, 1).start()

            for j in range(right_count):
                held[p, slot, j] = slots[last_ref[SPAN + j]]

            @pl.when(c > 0)
            def _():
                finish(c - 1, p)
        return carry

    lax.fori_loop(0, chunks, step, 0)
    for p in range(2):
        finish(chunks - 1, p)

    def drain(c, carry):
        for p in range(2):
            @pl.when(b > 0)
            def _():
                edge_copy(c, p, 0).wait_send()

            @pl.when(b < rb_size - 1)
            def _():
                edge_copy(c, p, 1).wait_send()
        return carry

    lax.fori_loop(0, chunks, drain, 0)

    @pl.when(a > 0)
    def _():
        halo_copy(0).wait_send()

    @pl.when(a < lb_size - 1)
    def _():
        halo_copy(1).wait_send()


def on_device(lb_size, rb_size, psi, left_env, right_env, left_src, right_dst):
    rows, cols = psi.shape
    terms = left_env.shape[0]
    left_count, right_count = rows // B, cols // B
    entries, targets = terms * right_count, right_count + 2 * SPAN
    groups = max_groups(entries, targets)
    chunks, width, halo = left_count // CHUNK, CHUNK * B, SPAN * B
    smem = pl.BlockSpec(memory_space=pltpu.SMEM)
    hbm = pl.BlockSpec(memory_space=pl.ANY)
    dma = pltpu.SemaphoreType.DMA
    edge = pltpu.VMEM((chunks, 2, halo, 2 * B), BF)
    return pl.pallas_call(
        functools.partial(main_kernel, (lb_size, rb_size, terms, left_count, right_count)),
        out_shape=pltpu.VMEM((rows, cols), BF),
        in_specs=[smem] * 2 + [hbm] * 3,
        out_specs=pl.BlockSpec(memory_space=pltpu.VMEM),
        scratch_shapes=[
            pltpu.VMEM((8, B), jnp.int32),
            pltpu.SMEM((8, B), jnp.int32),
            pltpu.SMEM((targets,), jnp.int32),
            pltpu.VMEM((rows, cols), BF),
            pltpu.VMEM((halo, cols), BF),
            pltpu.VMEM((halo, cols), BF),
            pltpu.VMEM((left_count + 2 * SPAN, cols, B), BF),
            pltpu.VMEM((terms, cols, B), BF),
            pltpu.VMEM((entries + 1, B, B), BF),
            pltpu.VMEM((2, terms, width, B), BF),
            pltpu.VMEM((entries, B, width), BF),
            pltpu.VMEM((groups + 1, B, 2 * B), F32),
            pltpu.VMEM((2, 2, right_count, B, 2 * B), F32),
            edge, edge, edge, edge,
            dma(()), dma(()), dma(()), dma((2, 2)), dma((2,)), dma((2,)), dma((2, chunks, 2)), dma((2, chunks, 2)),
        ],
        compiler_params=pltpu.CompilerParams(
            collective_id=0, has_side_effects=True, vmem_limit_bytes=54 * 2**20),
        name="apply",
    )(left_src, right_dst, psi, left_env, right_env)


def solution(mesh):
    return jax.shard_map(
        functools.partial(on_device, mesh.shape["lb"], mesh.shape["rb"]),
        mesh=mesh,
        in_specs=(P("lb", "rb"), P(None, "lb", None), P(None, "rb", None), P(), P()),
        out_specs=P("lb", "rb"),
        check_vma=False,
    )
```

```python
import functools

import jax
import jax.numpy as jnp
from jax import lax
from jax.experimental import pallas as pl
from jax.experimental.pallas import tpu as pltpu
from jax.sharding import PartitionSpec as P

SPAN = 2
B = 128
GROUP = 2
CHUNK = 4
LISTED = 256
MESH = pl.DeviceIdType.MESH
BF = jnp.bfloat16
F32 = jnp.float32


def max_groups(entries, targets):
    return (entries + (GROUP - 1) * targets) // GROUP


def plan(terms, right_count, start, dst_ref, list_v, last_ref):
    targets = right_count + 2 * SPAN
    entries = terms * right_count
    groups = max_groups(entries, targets)

    def target(w, j):
        return dst_ref[w, start + j] - start + SPAN

    def tally(w, counts):
        for j in range(right_count):
            d = target(w, j)
            counts = tuple(
                jnp.where(d == k, n + 1, n) if j <= k <= j + 2 * SPAN else n for k, n in enumerate(counts))
        return counts

    zeros = (jnp.int32(0),) * targets
    counts = lax.fori_loop(0, terms, tally, zeros)
    place = lax.broadcasted_iota(jnp.int32, (8, B), 0) * B + lax.broadcasted_iota(jnp.int32, (8, B), 1)
    listed = jnp.where(place < LISTED, entries, 1)
    begin = jnp.int32(0)
    begins = []
    for k, n in enumerate(counts):
        begins.append(begin * GROUP)
        listed = jnp.where(place == LISTED + begin, 0, listed)
        begin = begin + (n + GROUP - 1) // GROUP
        last_ref[k] = jnp.where(n > 0, begin - 1, groups)

    def put(w, carry):
        nexts, listed = carry
        for j in range(right_count):
            d = target(w, j)
            at = nexts[j]
            for k in range(j + 1, j + 2 * SPAN + 1):
                at = jnp.where(d == k, nexts[k], at)
            nexts = tuple(
                jnp.where(d == k, n + 1, n) if j <= k <= j + 2 * SPAN else n for k, n in enumerate(nexts))
            listed = jnp.where(place == at, w * right_count + j, listed)
        return nexts, listed

    _, listed = lax.fori_loop(0, terms, put, (tuple(begins), listed))
    list_v[...] = listed


def main_kernel(
    sizes, src, dst, psi, left, right, out,
    src_ref, dst_ref, list_v, list_s, last_ref, low_v, high_v, psi_t, right_t, left_v, inner, slots,
    send_down, send_up, from_below, from_above,
    index_sem, list_sem, psi_sem, right_sem, left_sem, halo_send, halo_recv, edge_send, edge_recv,
):
    lb_size, rb_size, terms, left_count, right_count = sizes
    targets = right_count + 2 * SPAN
    entries = terms * right_count
    groups = max_groups(entries, targets)
    rows, cols = left_count * B, right_count * B
    width = CHUNK * B
    chunks = left_count // CHUNK
    halo = SPAN * B
    a, b = lax.axis_index("lb"), lax.axis_index("rb")
    neighbours = (
        (a > 0, {"lb": a - 1}), (a < lb_size - 1, {"lb": a + 1}),
        (b > 0, {"rb": b - 1}), (b < rb_size - 1, {"rb": b + 1}),
    )

    psi_copy = pltpu.make_async_copy(psi, out, psi_sem)
    src_copy = pltpu.make_async_copy(src, src_ref, index_sem.at[0])
    dst_copy = pltpu.make_async_copy(dst, dst_ref, index_sem.at[1])
    right_copy = pltpu.make_async_copy(right, left_v.at[1], right_sem)
    list_copy = pltpu.make_async_copy(list_v, list_s, list_sem)

    def rows_of(c, p):
        return pl.multiple_of(lax.rem(halo + c * width + p * 2 * B, rows), 2 * B)

    def left_copy(c, p):
        return pltpu.make_async_copy(
            left.at[:, pl.ds(rows_of(c, p), 2 * B)],
            left_v.at[lax.rem(c, 2), :, pl.ds(p * 2 * B, 2 * B)],
            left_sem.at[lax.rem(c, 2), p],
        )

    def halo_copy(side):
        if side == 0:
            return pltpu.make_async_remote_copy(
                src_ref=psi.at[pl.ds(0, halo)], dst_ref=high_v, send_sem=halo_send.at[0],
                recv_sem=halo_recv.at[0], device_id={"lb": a - 1}, device_id_type=MESH)
        return pltpu.make_async_remote_copy(
            src_ref=psi.at[pl.ds(rows - halo, halo)], dst_ref=low_v, send_sem=halo_send.at[1],
            recv_sem=halo_recv.at[1], device_id={"lb": a + 1}, device_id_type=MESH)

    def edge_copy(c, p, side):
        if side == 0:
            return pltpu.make_async_remote_copy(
                src_ref=send_down.at[c, p], dst_ref=from_above.at[c, p], send_sem=edge_send.at[0, c, p],
                recv_sem=edge_recv.at[0, c, p], device_id={"rb": b - 1}, device_id_type=MESH)
        return pltpu.make_async_remote_copy(
            src_ref=send_up.at[c, p], dst_ref=from_below.at[c, p], send_sem=edge_send.at[1, c, p],
            recv_sem=edge_recv.at[1, c, p], device_id={"rb": b + 1}, device_id_type=MESH)

    dst_copy.start()
    psi_copy.start()
    src_copy.start()
    right_copy.start()
    for p in range(2):
        left_copy(0, p).start()

    barrier = pltpu.get_barrier_semaphore()
    for there, device in neighbours:
        @pl.when(there)
        def _():
            pl.semaphore_signal(barrier, inc=1, device_id=device, device_id_type=MESH)
    @pl.when(b == 0)
    def _():
        from_below[...] = jnp.zeros_like(from_below)

    @pl.when(b == rb_size - 1)
    def _():
        from_above[...] = jnp.zeros_like(from_above)

    right_t[entries] = jnp.zeros((B, B), BF)
    for p in range(2):
        slots[p, groups] = jnp.zeros((B, 2 * B), F32)

    dst_copy.wait()
    plan(terms, right_count, b * right_count, dst_ref, list_v, last_ref)
    list_copy.start()
    psi_copy.wait()

    def turn_psi(s, carry):
        for u in range(4):
            at = pl.multiple_of((4 * s + u) * B, B)
            psi_t[4 * s + u + SPAN] = out[pl.ds(at, B), :].T
        return carry

    lax.fori_loop(0, left_count // 4, turn_psi, 0)
    right_copy.wait()

    def turn_right(w, carry):
        for u in range(4):
            for j in range(right_count):
                right_t[(4 * w + u) * right_count + j] = left_v[1, 4 * w + u, pl.ds(j * B, B), :].T
        return carry

    lax.fori_loop(0, terms // 4, turn_right, 0)

    src_copy.wait()
    pl.semaphore_wait(barrier, sum(there.astype(jnp.int32) for there, _ in neighbours))

    @pl.when(a > 0)
    def _():
        halo_copy(0).start()

    @pl.when(a < lb_size - 1)
    def _():
        halo_copy(1).start()

    zero = jnp.zeros((B, B), BF)

    def finish(c, p):
        @pl.when(b > 0)
        def _():
            edge_copy(c, p, 1).wait_recv()

        @pl.when(b < rb_size - 1)
        def _():
            edge_copy(c, p, 0).wait_recv()

        for j in range(right_count):
            mine = slots[p, last_ref[SPAN + j]]
            if j < SPAN:
                mine = mine + from_below[c, p, pl.ds(j * B, B), :].astype(F32)
            if j >= right_count - SPAN:
                mine = mine + from_above[c, p, pl.ds((j - right_count + SPAN) * B, B), :].astype(F32)
            out[pl.ds(rows_of(c, p), 2 * B), pl.ds(j * B, B)] = mine.astype(BF).T

    def step(c, carry):
        for p in range(2):
            left_copy(c, p).wait()

        @pl.when(c < chunks - 1)
        def _():
            for p in range(2):
                left_copy(c + 1, p).start()

        @pl.when(c == chunks - 1)
        def _():
            @pl.when(a > 0)
            def _():
                halo_copy(1).wait_recv()
                for k in range(SPAN):
                    psi_t[k] = low_v[pl.ds(k * B, B), :].T

            @pl.when(a < lb_size - 1)
            def _():
                halo_copy(0).wait_recv()
                for k in range(SPAN):
                    psi_t[SPAN + left_count + k] = high_v[pl.ds(k * B, B), :].T

        first = a * left_count
        slot = lax.rem(c, 2)
        for w in range(terms):
            for p in range(2):
                i = first + lax.rem(SPAN + c * CHUNK + 2 * p, left_count)
                shift = SPAN - first
                x = jnp.concatenate(
                    [psi_t[jnp.clip(src_ref[w, i + k] + shift, 0, left_count + 2 * SPAN - 1)] for k in range(2)],
                    axis=1)
                upper = left_v[slot, w, pl.ds(p * 2 * B, B), :].T
                lower = left_v[slot, w, pl.ds(p * 2 * B + B, B), :].T
                both = jnp.concatenate(
                    [jnp.concatenate([upper, zero], axis=1), jnp.concatenate([zero, lower], axis=1)], axis=0)
                y = jnp.dot(x, both, preferred_element_type=F32).astype(BF)
                for j in range(right_count):
                    inner[w * right_count + j, :, pl.ds(p * 2 * B, 2 * B)] = y[j * B : (j + 1) * B]

        @pl.when(c == 0)
        def _():
            list_copy.wait()

        def pair(n):
            return list_s[n // B, n % B]

        for p in range(2):
            @pl.when(c > 0)
            def _():
                finish(c - 1, p)

            for g in range(groups):
                at = [pair(GROUP * g + q) for q in range(GROUP)]
                k = jnp.concatenate(
                    [inner[jnp.clip(e, 0, entries - 1), :, pl.ds(p * 2 * B, 2 * B)] for e in at], axis=0)
                r = jnp.concatenate([right_t[e] for e in at], axis=1)
                y = jnp.dot(r, k, preferred_element_type=F32)
                if g > 0:
                    y = y + jnp.where(pair(LISTED + g) == 1, slots[p, g - 1], 0.0)
                slots[p, g] = y
            for k in range(SPAN):
                send_down[c, p, pl.ds(k * B, B), :] = slots[p, last_ref[k]].astype(BF)
                send_up[c, p, pl.ds(k * B, B), :] = slots[p, last_ref[SPAN + right_count + k]].astype(BF)

            @pl.when(b > 0)
            def _():
                edge_copy(c, p, 0).start()

            @pl.when(b < rb_size - 1)
            def _():
                edge_copy(c, p, 1).start()

        return carry

    lax.fori_loop(0, chunks, step, 0)
    for p in range(2):
        finish(chunks - 1, p)

    def drain(c, carry):
        for p in range(2):
            @pl.when(b > 0)
            def _():
                edge_copy(c, p, 0).wait_send()

            @pl.when(b < rb_size - 1)
            def _():
                edge_copy(c, p, 1).wait_send()
        return carry

    lax.fori_loop(0, chunks, drain, 0)

    @pl.when(a > 0)
    def _():
        halo_copy(0).wait_send()

    @pl.when(a < lb_size - 1)
    def _():
        halo_copy(1).wait_send()


def on_device(lb_size, rb_size, psi, left_env, right_env, left_src, right_dst):
    rows, cols = psi.shape
    terms = left_env.shape[0]
    left_count, right_count = rows // B, cols // B
    entries, targets = terms * right_count, right_count + 2 * SPAN
    groups = max_groups(entries, targets)
    chunks, width, halo = left_count // CHUNK, CHUNK * B, SPAN * B
    hbm = pl.BlockSpec(memory_space=pl.ANY)
    dma = pltpu.SemaphoreType.DMA
    edge = pltpu.VMEM((chunks, 2, halo, 2 * B), BF)
    return pl.pallas_call(
        functools.partial(main_kernel, (lb_size, rb_size, terms, left_count, right_count)),
        out_shape=pltpu.VMEM((rows, cols), BF),
        in_specs=[hbm] * 5,
        out_specs=pl.BlockSpec(memory_space=pltpu.VMEM),
        scratch_shapes=[
            pltpu.SMEM(left_src.shape, jnp.int32),
            pltpu.SMEM(right_dst.shape, jnp.int32),
            pltpu.VMEM((8, B), jnp.int32),
            pltpu.SMEM((8, B), jnp.int32),
            pltpu.SMEM((targets,), jnp.int32),
            pltpu.VMEM((halo, cols), BF),
            pltpu.VMEM((halo, cols), BF),
            pltpu.VMEM((left_count + 2 * SPAN, cols, B), BF),
            pltpu.VMEM((entries + 1, B, B), BF),
            pltpu.VMEM((2, terms, width, B), BF),
            pltpu.VMEM((entries, B, width), BF),
            pltpu.VMEM((2, groups + 1, B, 2 * B), F32),
            edge, edge, edge, edge,
            dma((2,)), dma(()), dma(()), dma(()), dma((2, 2)), dma((2,)), dma((2,)), dma((2, chunks, 2)), dma((2, chunks, 2)),
        ],
        compiler_params=pltpu.CompilerParams(
            collective_id=0, has_side_effects=True, vmem_limit_bytes=54 * 2**20),
        name="apply",
    )(left_src, right_dst, psi, left_env, right_env)


def solution(mesh):
    return jax.shard_map(
        functools.partial(on_device, mesh.shape["lb"], mesh.shape["rb"]),
        mesh=mesh,
        in_specs=(P("lb", "rb"), P(None, "lb", None), P(None, "rb", None), P(), P()),
        out_specs=P("lb", "rb"),
        check_vma=False,
    )
```

```python
import functools

import jax
import jax.numpy as jnp
from jax import lax
from jax.experimental import pallas as pl
from jax.experimental.pallas import tpu as pltpu
from jax.sharding import PartitionSpec as P

SPAN = 2
B = 128
GROUP = 2
CHUNK = 4
LISTED = 256
MESH = pl.DeviceIdType.MESH
BF = jnp.bfloat16
F32 = jnp.float32


def max_groups(entries, targets):
    return (entries + (GROUP - 1) * targets) // GROUP


def plan(terms, right_count, start, odd, dst_ref, list_v, last_ref):
    targets = right_count + 2 * SPAN
    entries = terms * right_count
    groups = max_groups(entries, targets)

    blocks = [jnp.where(odd, right_count - 1 - j, j) for j in range(right_count)]
    sign, base = jnp.where(odd, -1, 1), jnp.where(odd, targets - 1 - SPAN + start, SPAN - start)

    def target(w, j):
        return base + sign * dst_ref[w, start + blocks[j]]

    def tally(w, counts):
        for j in range(right_count):
            d = target(w, j)
            counts = tuple(
                jnp.where(d == k, n + 1, n) if j <= k <= j + 2 * SPAN else n for k, n in enumerate(counts))
        return counts

    zeros = (jnp.int32(0),) * targets
    counts = lax.fori_loop(0, terms, tally, zeros)
    place = lax.broadcasted_iota(jnp.int32, (8, B), 0) * B + lax.broadcasted_iota(jnp.int32, (8, B), 1)
    listed = jnp.where(place < LISTED, entries, 1)
    begin = jnp.int32(0)
    begins = []
    for k, n in enumerate(counts):
        begins.append(begin * GROUP)
        listed = jnp.where(place == LISTED + begin, 0, listed)
        begin = begin + (n + GROUP - 1) // GROUP
        last_ref[k] = jnp.where(n > 0, begin - 1, groups)

    def put(w, carry):
        nexts, listed = carry
        for j in range(right_count):
            d = target(w, j)
            at = nexts[j]
            for k in range(j + 1, j + 2 * SPAN + 1):
                at = jnp.where(d == k, nexts[k], at)
            nexts = tuple(
                jnp.where(d == k, n + 1, n) if j <= k <= j + 2 * SPAN else n for k, n in enumerate(nexts))
            listed = jnp.where(place == at, w * right_count + blocks[j], listed)
        return nexts, listed

    _, listed = lax.fori_loop(0, terms, put, (tuple(begins), listed))
    list_v[...] = listed


def main_kernel(
    sizes, src, dst, psi, left, right, out,
    src_ref, dst_ref, list_v, list_s, last_ref, low_v, high_v, psi_t, right_t, left_v, inner, slots,
    send_outer, send_inner, arrived,
    index_sem, list_sem, psi_sem, right_sem, left_sem, halo_send, halo_recv, edge_send, edge_recv,
):
    lb_size, rb_size, terms, left_count, right_count = sizes
    targets = right_count + 2 * SPAN
    entries = terms * right_count
    groups = max_groups(entries, targets)
    rows, cols = left_count * B, right_count * B
    width = CHUNK * B
    chunks = left_count // CHUNK
    halo = SPAN * B
    a, b = lax.axis_index("lb"), lax.axis_index("rb")
    early = max_groups(SPAN * terms, SPAN)
    odd = lax.rem(b, 2) == 1
    outer, inner_b = jnp.where(odd, b + 1, b - 1), jnp.where(odd, b - 1, b + 1)
    has_outer = (b > 0) & (b < rb_size - 1)
    neighbours = (
        (a > 0, {"lb": a - 1}), (a < lb_size - 1, {"lb": a + 1}),
        (has_outer, {"rb": outer}), (b >= 0, {"rb": inner_b}),
    )

    psi_copy = pltpu.make_async_copy(psi, out, psi_sem)
    src_copy = pltpu.make_async_copy(src, src_ref, index_sem.at[0])
    dst_copy = pltpu.make_async_copy(dst, dst_ref, index_sem.at[1])
    right_copy = pltpu.make_async_copy(right, left_v.at[1], right_sem)
    list_copy = pltpu.make_async_copy(list_v, list_s, list_sem)

    def rows_of(c, p):
        return pl.multiple_of(lax.rem(halo + c * width + p * 2 * B, rows), 2 * B)

    def left_copy(c, p):
        return pltpu.make_async_copy(
            left.at[:, pl.ds(rows_of(c, p), 2 * B)],
            left_v.at[lax.rem(c, 2), :, pl.ds(p * 2 * B, 2 * B)],
            left_sem.at[lax.rem(c, 2), p],
        )

    def halo_copy(side):
        if side == 0:
            return pltpu.make_async_remote_copy(
                src_ref=psi.at[pl.ds(0, halo)], dst_ref=high_v, send_sem=halo_send.at[0],
                recv_sem=halo_recv.at[0], device_id={"lb": a - 1}, device_id_type=MESH)
        return pltpu.make_async_remote_copy(
            src_ref=psi.at[pl.ds(rows - halo, halo)], dst_ref=low_v, send_sem=halo_send.at[1],
            recv_sem=halo_recv.at[1], device_id={"lb": a + 1}, device_id_type=MESH)

    def outer_copy(c, p):
        return pltpu.make_async_remote_copy(
            src_ref=send_outer.at[c, p], dst_ref=arrived.at[jnp.where(odd, 0, 1), c, p],
            send_sem=edge_send.at[0, c, p], recv_sem=edge_recv.at[0, c, p],
            device_id={"rb": outer}, device_id_type=MESH)

    def inner_copy(c, p):
        return pltpu.make_async_remote_copy(
            src_ref=send_inner.at[c, p], dst_ref=arrived.at[jnp.where(odd, 1, 0), c, p],
            send_sem=edge_send.at[1, c, p], recv_sem=edge_recv.at[1, c, p],
            device_id={"rb": inner_b}, device_id_type=MESH)

    dst_copy.start()
    psi_copy.start()
    src_copy.start()
    right_copy.start()

    barrier = pltpu.get_barrier_semaphore()
    for there, device in neighbours:
        @pl.when(there)
        def _():
            pl.semaphore_signal(barrier, inc=1, device_id=device, device_id_type=MESH)
    @pl.when(b == 0)
    def _():
        arrived[0] = jnp.zeros(arrived.shape[1:], BF)

    @pl.when(b == rb_size - 1)
    def _():
        arrived[1] = jnp.zeros(arrived.shape[1:], BF)

    right_t[entries] = jnp.zeros((B, B), BF)
    for p in range(2):
        slots[p, groups] = jnp.zeros((B, 2 * B), F32)

    dst_copy.wait()
    plan(terms, right_count, b * right_count, odd, dst_ref, list_v, last_ref)
    list_copy.start()
    for p in range(2):
        left_copy(0, p).start()
    psi_copy.wait()

    def turn_psi(s, carry):
        for u in range(8):
            at = pl.multiple_of((8 * s + u) * B, B)
            psi_t[8 * s + u + SPAN] = out[pl.ds(at, B), :].T
        return carry

    lax.fori_loop(0, left_count // 8, turn_psi, 0)
    right_copy.wait()

    def turn_right(w, carry):
        for u in range(14):
            for j in range(right_count):
                right_t[(14 * w + u) * right_count + j] = left_v[1, 14 * w + u, pl.ds(j * B, B), :].T
        return carry

    lax.fori_loop(0, terms // 14, turn_right, 0)

    src_copy.wait()
    list_copy.wait()
    pl.semaphore_wait(barrier, sum(there.astype(jnp.int32) for there, _ in neighbours))

    @pl.when(a > 0)
    def _():
        halo_copy(0).start()

    @pl.when(a < lb_size - 1)
    def _():
        halo_copy(1).start()

    zero = jnp.zeros((B, B), BF)

    def finish(c, p):
        inner_copy(c, p).wait_recv()

        @pl.when(has_outer)
        def _():
            outer_copy(c, p).wait_recv()

        for j in range(right_count):
            mine = slots[p, last_ref[jnp.where(odd, targets - 1 - SPAN - j, SPAN + j)]]
            if j < SPAN:
                mine = mine + arrived[0, c, p, pl.ds(j * B, B), :].astype(F32)
            if j >= right_count - SPAN:
                mine = mine + arrived[1, c, p, pl.ds((j - right_count + SPAN) * B, B), :].astype(F32)
            out[pl.ds(rows_of(c, p), 2 * B), pl.ds(j * B, B)] = mine.astype(BF).T

    def step(c, carry):
        for p in range(2):
            left_copy(c, p).wait()

        @pl.when(c < chunks - 1)
        def _():
            for p in range(2):
                left_copy(c + 1, p).start()

        @pl.when(c == chunks - 1)
        def _():
            @pl.when(a > 0)
            def _():
                halo_copy(1).wait_recv()
                for k in range(SPAN):
                    psi_t[k] = low_v[pl.ds(k * B, B), :].T

            @pl.when(a < lb_size - 1)
            def _():
                halo_copy(0).wait_recv()
                for k in range(SPAN):
                    psi_t[SPAN + left_count + k] = high_v[pl.ds(k * B, B), :].T

        first = a * left_count
        slot = lax.rem(c, 2)
        for w in range(terms):
            for p in range(2):
                i = first + lax.rem(SPAN + c * CHUNK + 2 * p, left_count)
                shift = SPAN - first
                x = jnp.concatenate(
                    [psi_t[jnp.clip(src_ref[w, i + k] + shift, 0, left_count + 2 * SPAN - 1)] for k in range(2)],
                    axis=1)
                upper = left_v[slot, w, pl.ds(p * 2 * B, B), :].T
                lower = left_v[slot, w, pl.ds(p * 2 * B + B, B), :].T
                both = jnp.concatenate(
                    [jnp.concatenate([upper, zero], axis=1), jnp.concatenate([zero, lower], axis=1)], axis=0)
                y = jnp.dot(x, both, preferred_element_type=F32).astype(BF)
                for j in range(right_count):
                    inner[w * right_count + j, :, pl.ds(p * 2 * B, 2 * B)] = y[j * B : (j + 1) * B]

        def pair(n):
            return list_s[n // B, n % B]

        def right_product(p, begin, end):
            for g in range(begin, end):
                at = [pair(GROUP * g + q) for q in range(GROUP)]
                k = jnp.concatenate(
                    [inner[jnp.clip(e, 0, entries - 1), :, pl.ds(p * 2 * B, 2 * B)] for e in at], axis=0)
                r = jnp.concatenate([right_t[e] for e in at], axis=1)
                y = jnp.dot(r, k, preferred_element_type=F32)
                if g > 0:
                    y = y + jnp.where(pair(LISTED + g) == 1, slots[p, g - 1], 0.0)
                slots[p, g] = y

        def before(p):
            @pl.when(c > 0)
            def _():
                finish(c - 1, p)

        def to_outer(p):
            for k in range(SPAN):
                send_outer[c, p, pl.ds(k * B, B), :] = slots[p, last_ref[jnp.where(odd, SPAN - 1 - k, k)]].astype(BF)

            @pl.when(has_outer)
            def _():
                outer_copy(c, p).start()

        def to_inner(p):
            for k in range(SPAN):
                at = last_ref[jnp.where(odd, targets - 1 - k, targets - SPAN + k)]
                send_inner[c, p, pl.ds(k * B, B), :] = slots[p, at].astype(BF)
            inner_copy(c, p).start()

        @pl.when(c < chunks - 1)
        def _():
            for p in range(2):
                before(p)
                right_product(p, 0, groups)
                to_outer(p)
                to_inner(p)

        @pl.when(c == chunks - 1)
        def _():
            for p in range(2):
                before(p)
                right_product(p, 0, early)
                to_outer(p)
            for p in range(2):
                right_product(p, early, groups)
                to_inner(p)
        return carry

    lax.fori_loop(0, chunks, step, 0)
    for p in range(2):
        finish(chunks - 1, p)

    def drain(c, carry):
        for p in range(2):
            inner_copy(c, p).wait_send()

            @pl.when(has_outer)
            def _():
                outer_copy(c, p).wait_send()
        return carry

    lax.fori_loop(0, chunks, drain, 0)

    @pl.when(a > 0)
    def _():
        halo_copy(0).wait_send()

    @pl.when(a < lb_size - 1)
    def _():
        halo_copy(1).wait_send()


def on_device(lb_size, rb_size, psi, left_env, right_env, left_src, right_dst):
    rows, cols = psi.shape
    terms = left_env.shape[0]
    left_count, right_count = rows // B, cols // B
    entries, targets = terms * right_count, right_count + 2 * SPAN
    groups = max_groups(entries, targets)
    chunks, width, halo = left_count // CHUNK, CHUNK * B, SPAN * B
    hbm = pl.BlockSpec(memory_space=pl.ANY)
    dma = pltpu.SemaphoreType.DMA
    edge = pltpu.VMEM((chunks, 2, halo, 2 * B), BF)
    return pl.pallas_call(
        functools.partial(main_kernel, (lb_size, rb_size, terms, left_count, right_count)),
        out_shape=pltpu.VMEM((rows, cols), BF),
        in_specs=[hbm] * 5,
        out_specs=pl.BlockSpec(memory_space=pltpu.VMEM),
        scratch_shapes=[
            pltpu.SMEM(left_src.shape, jnp.int32),
            pltpu.SMEM(right_dst.shape, jnp.int32),
            pltpu.VMEM((8, B), jnp.int32),
            pltpu.SMEM((8, B), jnp.int32),
            pltpu.SMEM((targets,), jnp.int32),
            pltpu.VMEM((halo, cols), BF),
            pltpu.VMEM((halo, cols), BF),
            pltpu.VMEM((left_count + 2 * SPAN, cols, B), BF),
            pltpu.VMEM((entries + 1, B, B), BF),
            pltpu.VMEM((2, terms, width, B), BF),
            pltpu.VMEM((entries, B, width), BF),
            pltpu.VMEM((2, groups + 1, B, 2 * B), F32),
            edge, edge, pltpu.VMEM((2, chunks, 2, halo, 2 * B), BF),
            dma((2,)), dma(()), dma(()), dma(()), dma((2, 2)), dma((2,)), dma((2,)), dma((2, chunks, 2)), dma((2, chunks, 2)),
        ],
        compiler_params=pltpu.CompilerParams(
            collective_id=0, has_side_effects=True, vmem_limit_bytes=54 * 2**20),
        name="apply",
    )(left_src, right_dst, psi, left_env, right_env)


def solution(mesh):
    return jax.shard_map(
        functools.partial(on_device, mesh.shape["lb"], mesh.shape["rb"]),
        mesh=mesh,
        in_specs=(P("lb", "rb"), P(None, "lb", None), P(None, "rb", None), P(), P()),
        out_specs=P("lb", "rb"),
        check_vma=False,
    )
```

```python
import functools

import jax
import jax.numpy as jnp
from jax import lax
from jax.experimental import pallas as pl
from jax.experimental.pallas import tpu as pltpu
from jax.sharding import PartitionSpec as P

SPAN = 2
B = 128
GROUP = 2
CHUNK = 4
LISTED = 256
MESH = pl.DeviceIdType.MESH
BF = jnp.bfloat16
F32 = jnp.float32


def max_groups(entries, targets):
    return (entries + (GROUP - 1) * targets) // GROUP


def plan(terms, right_count, start, odd, dst_ref, list_v, last_ref):
    targets = right_count + 2 * SPAN
    entries = terms * right_count
    groups = max_groups(entries, targets)

    blocks = [jnp.where(odd, right_count - 1 - j, j) for j in range(right_count)]
    sign, base = jnp.where(odd, -1, 1), jnp.where(odd, targets - 1 - SPAN + start, SPAN - start)

    def target(w, j):
        return base + sign * dst_ref[w, start + blocks[j]]

    def tally(w, counts):
        for j in range(right_count):
            d = target(w, j)
            counts = tuple(
                jnp.where(d == k, n + 1, n) if j <= k <= j + 2 * SPAN else n for k, n in enumerate(counts))
        return counts

    zeros = (jnp.int32(0),) * targets
    counts = lax.fori_loop(0, terms, tally, zeros)
    place = lax.broadcasted_iota(jnp.int32, (8, B), 0) * B + lax.broadcasted_iota(jnp.int32, (8, B), 1)
    listed = jnp.where(place < LISTED, entries, 1)
    begin = jnp.int32(0)
    begins = []
    for k, n in enumerate(counts):
        begins.append(begin * GROUP)
        listed = jnp.where(place == LISTED + begin, 0, listed)
        begin = begin + (n + GROUP - 1) // GROUP
        last_ref[k] = jnp.where(n > 0, begin - 1, groups)

    def put(w, carry):
        nexts, listed = carry
        for j in range(right_count):
            d = target(w, j)
            at = nexts[j]
            for k in range(j + 1, j + 2 * SPAN + 1):
                at = jnp.where(d == k, nexts[k], at)
            nexts = tuple(
                jnp.where(d == k, n + 1, n) if j <= k <= j + 2 * SPAN else n for k, n in enumerate(nexts))
            listed = jnp.where(place == at, w * right_count + blocks[j], listed)
        return nexts, listed

    _, listed = lax.fori_loop(0, terms, put, (tuple(begins), listed))
    list_v[...] = listed


def main_kernel(
    sizes, src, dst, psi, left, right, out,
    src_ref, dst_ref, list_v, list_s, last_ref, low_v, high_v, psi_t, right_t, left_v, inner, slots,
    send_outer, send_inner, arrived,
    index_sem, list_sem, psi_sem, right_sem, left_sem, halo_send, halo_recv, edge_send, edge_recv,
):
    lb_size, rb_size, terms, left_count, right_count = sizes
    targets = right_count + 2 * SPAN
    entries = terms * right_count
    groups = max_groups(entries, targets)
    rows, cols = left_count * B, right_count * B
    width = CHUNK * B
    chunks = left_count // CHUNK
    halo = SPAN * B
    a, b = lax.axis_index("lb"), lax.axis_index("rb")
    early = max_groups(SPAN * terms, SPAN)
    odd = lax.rem(b, 2) == 1
    outer, inner_b = jnp.where(odd, b + 1, b - 1), jnp.where(odd, b - 1, b + 1)
    has_outer = (b > 0) & (b < rb_size - 1)
    neighbours = (
        (a > 0, {"lb": a - 1}), (a < lb_size - 1, {"lb": a + 1}),
        (has_outer, {"rb": outer}), (b >= 0, {"rb": inner_b}),
    )

    psi_copy = pltpu.make_async_copy(psi, out, psi_sem)
    src_copy = pltpu.make_async_copy(src, src_ref, index_sem.at[0])
    dst_copy = pltpu.make_async_copy(dst, dst_ref, index_sem.at[1])
    right_copy = pltpu.make_async_copy(right, left_v.at[1], right_sem)
    list_copy = pltpu.make_async_copy(list_v, list_s, list_sem)

    def rows_of(c, p):
        return pl.multiple_of(lax.rem(halo + c * width + p * 2 * B, rows), 2 * B)

    def left_copy(c, p):
        return pltpu.make_async_copy(
            left.at[:, pl.ds(rows_of(c, p), 2 * B)],
            left_v.at[lax.rem(c, 2), :, pl.ds(p * 2 * B, 2 * B)],
            left_sem.at[lax.rem(c, 2), p],
        )

    def halo_copy(side):
        if side == 0:
            return pltpu.make_async_remote_copy(
                src_ref=psi.at[pl.ds(0, halo)], dst_ref=high_v, send_sem=halo_send.at[0],
                recv_sem=halo_recv.at[0], device_id={"lb": a - 1}, device_id_type=MESH)
        return pltpu.make_async_remote_copy(
            src_ref=psi.at[pl.ds(rows - halo, halo)], dst_ref=low_v, send_sem=halo_send.at[1],
            recv_sem=halo_recv.at[1], device_id={"lb": a + 1}, device_id_type=MESH)

    def outer_copy(c, p):
        return pltpu.make_async_remote_copy(
            src_ref=send_outer.at[c, p], dst_ref=arrived.at[jnp.where(odd, 0, 1), c, p],
            send_sem=edge_send.at[0, c, p], recv_sem=edge_recv.at[0, c, p],
            device_id={"rb": outer}, device_id_type=MESH)

    def inner_copy(c, p):
        return pltpu.make_async_remote_copy(
            src_ref=send_inner.at[c, p], dst_ref=arrived.at[jnp.where(odd, 1, 0), c, p],
            send_sem=edge_send.at[1, c, p], recv_sem=edge_recv.at[1, c, p],
            device_id={"rb": inner_b}, device_id_type=MESH)

    dst_copy.start()
    psi_copy.start()
    src_copy.start()
    right_copy.start()

    barrier = pltpu.get_barrier_semaphore()
    for there, device in neighbours:
        @pl.when(there)
        def _():
            pl.semaphore_signal(barrier, inc=1, device_id=device, device_id_type=MESH)
    @pl.when(b == 0)
    def _():
        arrived[0] = jnp.zeros(arrived.shape[1:], BF)

    @pl.when(b == rb_size - 1)
    def _():
        arrived[1] = jnp.zeros(arrived.shape[1:], BF)

    right_t[entries] = jnp.zeros((B, B), BF)
    for p in range(2):
        slots[p, groups] = jnp.zeros((B, 2 * B), F32)

    dst_copy.wait()
    plan(terms, right_count, b * right_count, odd, dst_ref, list_v, last_ref)
    list_copy.start()
    for p in range(2):
        left_copy(0, p).start()
    psi_copy.wait()

    def turn_psi(s, carry):
        for u in range(8):
            at = pl.multiple_of((8 * s + u) * B, B)
            psi_t[8 * s + u + SPAN] = out[pl.ds(at, B), :].T
        return carry

    lax.fori_loop(0, left_count // 8, turn_psi, 0)
    right_copy.wait()

    def turn_right(w, carry):
        for u in range(14):
            for j in range(right_count):
                right_t[(14 * w + u) * right_count + j] = left_v[1, 14 * w + u, pl.ds(j * B, B), :].T
        return carry

    lax.fori_loop(0, terms // 14, turn_right, 0)

    src_copy.wait()
    list_copy.wait()
    pl.semaphore_wait(barrier, sum(there.astype(jnp.int32) for there, _ in neighbours))

    @pl.when(a > 0)
    def _():
        halo_copy(0).start()

    @pl.when(a < lb_size - 1)
    def _():
        halo_copy(1).start()

    zero = jnp.zeros((B, B), BF)

    def finish(c, p):
        inner_copy(c, p).wait_recv()

        @pl.when(has_outer)
        def _():
            outer_copy(c, p).wait_recv()

        for j in range(right_count):
            mine = slots[p, last_ref[jnp.where(odd, targets - 1 - SPAN - j, SPAN + j)]]
            if j < SPAN:
                mine = mine + arrived[0, c, p, pl.ds(j * B, B), :].astype(F32)
            if j >= right_count - SPAN:
                mine = mine + arrived[1, c, p, pl.ds((j - right_count + SPAN) * B, B), :].astype(F32)
            out[pl.ds(rows_of(c, p), 2 * B), pl.ds(j * B, B)] = mine.astype(BF).T

    def step(c, carry):
        for p in range(2):
            left_copy(c, p).wait()

        @pl.when(c < chunks - 1)
        def _():
            for p in range(2):
                left_copy(c + 1, p).start()

        @pl.when(c == chunks - 1)
        def _():
            @pl.when(a > 0)
            def _():
                halo_copy(1).wait_recv()
                for k in range(SPAN):
                    psi_t[k] = low_v[pl.ds(k * B, B), :].T

            @pl.when(a < lb_size - 1)
            def _():
                halo_copy(0).wait_recv()
                for k in range(SPAN):
                    psi_t[SPAN + left_count + k] = high_v[pl.ds(k * B, B), :].T

        first = a * left_count
        slot = lax.rem(c, 2)
        for w in range(terms):
            for p in range(2):
                i = first + lax.rem(SPAN + c * CHUNK + 2 * p, left_count)
                shift = SPAN - first
                x = jnp.concatenate(
                    [psi_t[jnp.clip(src_ref[w, i + k] + shift, 0, left_count + 2 * SPAN - 1)] for k in range(2)],
                    axis=1)
                upper = left_v[slot, w, pl.ds(p * 2 * B, B), :].T
                lower = left_v[slot, w, pl.ds(p * 2 * B + B, B), :].T
                both = jnp.concatenate(
                    [jnp.concatenate([upper, zero], axis=1), jnp.concatenate([zero, lower], axis=1)], axis=0)
                y = jnp.dot(x, both, preferred_element_type=F32).astype(BF)
                for j in range(right_count):
                    inner[w * right_count + j, :, pl.ds(p * 2 * B, 2 * B)] = y[j * B : (j + 1) * B]

        def pair(n):
            return list_s[n // B, n % B]

        def right_product(p, begin, end):
            for g in range(begin, end):
                at = [pair(GROUP * g + q) for q in range(GROUP)]
                k = jnp.concatenate(
                    [inner[jnp.clip(e, 0, entries - 1), :, pl.ds(p * 2 * B, 2 * B)] for e in at], axis=0)
                r = jnp.concatenate([right_t[e] for e in at], axis=1)
                y = jnp.dot(r, k, preferred_element_type=F32)
                if g > 0:
                    y = y + jnp.where(pair(LISTED + g) == 1, slots[p, g - 1], 0.0)
                slots[p, g] = y

        def before(p):
            @pl.when(c > 0)
            def _():
                finish(c - 1, p)

        def fill_outer(p):
            for k in range(SPAN):
                send_outer[c, p, pl.ds(k * B, B), :] = slots[p, last_ref[jnp.where(odd, SPAN - 1 - k, k)]].astype(BF)

        def start_outer(p):
            @pl.when(has_outer)
            def _():
                outer_copy(c, p).start()

        def fill_inner(p):
            for k in range(SPAN):
                at = last_ref[jnp.where(odd, targets - 1 - k, targets - SPAN + k)]
                send_inner[c, p, pl.ds(k * B, B), :] = slots[p, at].astype(BF)

        @pl.when(c < chunks - 1)
        def _():
            for p in range(2):
                before(p)
                right_product(p, 0, groups)
                fill_outer(p)
                fill_inner(p)
                inner_copy(c, p).start()
                start_outer(p)

        @pl.when(c == chunks - 1)
        def _():
            for p in range(2):
                before(p)
                right_product(p, 0, early)
                fill_outer(p)
                start_outer(p)
            for p in range(2):
                right_product(p, early, groups)
                fill_inner(p)
                inner_copy(c, p).start()
        return carry

    lax.fori_loop(0, chunks, step, 0)
    for p in range(2):
        finish(chunks - 1, p)

    def drain(c, carry):
        for p in range(2):
            inner_copy(c, p).wait_send()

            @pl.when(has_outer)
            def _():
                outer_copy(c, p).wait_send()
        return carry

    lax.fori_loop(0, chunks, drain, 0)

    @pl.when(a > 0)
    def _():
        halo_copy(0).wait_send()

    @pl.when(a < lb_size - 1)
    def _():
        halo_copy(1).wait_send()


def on_device(lb_size, rb_size, psi, left_env, right_env, left_src, right_dst):
    rows, cols = psi.shape
    terms = left_env.shape[0]
    left_count, right_count = rows // B, cols // B
    entries, targets = terms * right_count, right_count + 2 * SPAN
    groups = max_groups(entries, targets)
    chunks, width, halo = left_count // CHUNK, CHUNK * B, SPAN * B
    hbm = pl.BlockSpec(memory_space=pl.ANY)
    dma = pltpu.SemaphoreType.DMA
    edge = pltpu.VMEM((chunks, 2, halo, 2 * B), BF)
    return pl.pallas_call(
        functools.partial(main_kernel, (lb_size, rb_size, terms, left_count, right_count)),
        out_shape=pltpu.VMEM((rows, cols), BF),
        in_specs=[hbm] * 5,
        out_specs=pl.BlockSpec(memory_space=pltpu.VMEM),
        scratch_shapes=[
            pltpu.SMEM(left_src.shape, jnp.int32),
            pltpu.SMEM(right_dst.shape, jnp.int32),
            pltpu.VMEM((8, B), jnp.int32),
            pltpu.SMEM((8, B), jnp.int32),
            pltpu.SMEM((targets,), jnp.int32),
            pltpu.VMEM((halo, cols), BF),
            pltpu.VMEM((halo, cols), BF),
            pltpu.VMEM((left_count + 2 * SPAN, cols, B), BF),
            pltpu.VMEM((entries + 1, B, B), BF),
            pltpu.VMEM((2, terms, width, B), BF),
            pltpu.VMEM((entries, B, width), BF),
            pltpu.VMEM((2, groups + 1, B, 2 * B), F32),
            edge, edge, pltpu.VMEM((2, chunks, 2, halo, 2 * B), BF),
            dma((2,)), dma(()), dma(()), dma(()), dma((2, 2)), dma((2,)), dma((2,)), dma((2, chunks, 2)), dma((2, chunks, 2)),
        ],
        compiler_params=pltpu.CompilerParams(
            collective_id=0, has_side_effects=True, vmem_limit_bytes=54 * 2**20),
        name="apply",
    )(left_src, right_dst, psi, left_env, right_env)


def solution(mesh):
    return jax.shard_map(
        functools.partial(on_device, mesh.shape["lb"], mesh.shape["rb"]),
        mesh=mesh,
        in_specs=(P("lb", "rb"), P(None, "lb", None), P(None, "rb", None), P(), P()),
        out_specs=P("lb", "rb"),
        check_vma=False,
    )
```
